1024 devices in a mesh: row: 32 (over z), col: 32 (over y, x, core).
Axes of the slice: x: 4, y: 4, z: 32, core: 2. Of those that a mesh axis runs over, the one named last changes fastest.
Arguments:
- density: bfloat16 [32768, 32768], P('row', 'col'), as said below
- occupancy: int32 [256, 256], P('row', 'col'), may hold values from 0 to 1, as said below
- product_keep: int32 [4, 256], replicated, may hold values 0 or 1
Outputs:
- purified: bfloat16 [512, 32768], P('row', 'col')
The draws below stay inside these ranges and needn't reach their ends.
Inputs may be any that keep to these rules, and one draw needn't show every extreme that they name: density is symmetric. occupancy is symmetric and every diagonal block is stored.
All inputs are finite; a program needn't handle non-finite values.
Results may differ from the reference program's by a relative error of at most 0.015.
Values may be sent and summed in bfloat16 or wider, within the bound.
No kernel may reach another device: no remote copies, remote signals or barrier semaphores. Data moves between devices by JAX's collectives and lax.ppermute only.
A program may use at most 32 MiB of HBM per device.

```python
import jax
import jax.numpy as jnp
from jax import lax

BS = 128
NB = 256
WB = 4
N = 32768
RW = 512


def draw_density(key, part):
    key = jax.random.fold_in(key, 11)
    index = jnp.arange(N)
    upper = index[:, None] <= index[None, :]
    base = jax.random.normal(key, (N, N), jnp.float32)
    symmetric = jnp.where(upper, base, base.T)
    return (0.04 * symmetric).astype(jnp.bfloat16)


def draw_occupancy(key, part):
    key = jax.random.fold_in(key, 23)
    scores = jax.random.randint(key, (NB, NB), 0, 1000)
    index = jnp.arange(NB)
    upper = index[:, None] <= index[None, :]
    distance = jnp.abs(index[:, None] - index[None, :])
    limit = jnp.maximum(150, 1000 - 8 * distance)
    symmetric = jnp.where(upper, scores, scores.T)
    return (symmetric < limit).astype(jnp.int32)


def place_ends(result, own_key, low, largest):
    shape = result.shape
    spot = [jax.random.randint(jax.random.fold_in(own_key, axis), (), 0, shape[axis]) for axis in range(len(shape))]
    result = result.at[tuple(spot)].set(low)
    longest = shape.index(max(shape))
    spot[longest] = (spot[longest] + 1) % shape[longest]
    return result.at[tuple(spot)].set(largest)


def setup_inputs(seed: int = 0) -> dict:
    keys = jax.random.split(jax.random.key(seed), 4)
    return {
        "density": draw_density(jax.random.fold_in(keys[3], 71), 0),
        "occupancy": draw_occupancy(jax.random.fold_in(keys[3], 71), 0),
        "product_keep": place_ends((jax.random.randint(keys[2], (WB, NB), 0, 4) < 3).astype(jnp.int32), jax.random.fold_in(keys[2], 1), 0, 1),
    }


def panel_product(left, density, occ_rows):
    def one_panel(block_index):
        panel = lax.dynamic_slice_in_dim(density, block_index * BS, BS, 1).astype(jnp.float32)
        stored = lax.dynamic_slice_in_dim(occ_rows, block_index, 1, 1).astype(jnp.float32)
        return jnp.dot(left, panel * stored, precision=lax.Precision.HIGHEST)

    panels = lax.map(one_panel, jnp.arange(NB, dtype=jnp.int32))
    return jnp.transpose(panels, (1, 0, 2)).reshape(left.shape[0], NB * BS)


def reference(density, occupancy, product_keep):
    occ_rows = jnp.repeat(occupancy, BS, axis=0)
    window_occ = jnp.repeat(occ_rows[:RW], BS, axis=1).astype(jnp.float32)
    window_left = density[:RW].astype(jnp.float32) * window_occ
    keep_full = jnp.repeat(jnp.repeat(product_keep, BS, axis=0), BS, axis=1).astype(jnp.float32)
    square = (panel_product(window_left, density, occ_rows) * keep_full).astype(jnp.bfloat16)
    square_wide = square.astype(jnp.float32)
    cube = panel_product(square_wide, density, occ_rows)
    return ((3.0 * square_wide - 2.0 * cube) * keep_full).astype(jnp.bfloat16)
```

```python
import functools

import jax
import jax.numpy as jnp
from jax import lax
from jax.experimental import pallas as pl
from jax.experimental.pallas import tpu as pltpu
from jax.sharding import PartitionSpec as P

BS = 128
BF16 = jnp.bfloat16
F32 = jnp.float32
VMEM = pl.BlockSpec(memory_space=pltpu.VMEM)
SMEM = pl.BlockSpec(memory_space=pltpu.SMEM)
BOTH = ("row", "col")


def call(kernel, outs, cost, scratch=()):
    return functools.partial(
        pl.pallas_call,
        kernel,
        out_shape=outs,
        out_specs=jax.tree.map(lambda _: VMEM, outs),
        scratch_shapes=list(scratch),
        compiler_params=pltpu.CompilerParams(vmem_limit_bytes=24 * 2**20),
        cost_estimate=pl.CostEstimate(flops=cost, bytes_accessed=4 * 2**20, transcendentals=0),
    )


def mask_kernel(where_ref, occ_ref, density_ref, sparse_ref, panel_ref):
    down, across = occ_ref.shape
    window = panel_ref.shape[0] // BS
    first = where_ref[0] == 0
    for i in range(down):
        for j in range(across):
            spot = (pl.ds(i * BS, BS), pl.ds(j * BS, BS))
            kept = density_ref[spot] * occ_ref[i, j].astype(F32).astype(BF16)
            sparse_ref[spot] = kept
            if i < window:
                panel_ref[spot] = jnp.where(first, kept, jnp.zeros_like(kept))


def square_kernel(where_ref, low_ref, high_ref, sparse_ref, kept_ref, sent_ref):
    core = where_ref[1] % 2
    tile = min(256, sparse_ref.shape[0])
    for n in range(0, sparse_ref.shape[0], tile):
        right = sparse_ref[pl.ds(n, tile), :]

        def product(left):
            return lax.dot_general(left, right, (((1,), (1,)), ((), ())), preferred_element_type=F32)

        low, high = product(low_ref[...]), product(high_ref[...])
        kept_ref[:, pl.ds(n, tile)] = jnp.where(core == 0, low, high)
        sent_ref[:, pl.ds(n, tile)] = jnp.where(core == 0, high, low).astype(BF16)


def cube_kernel(rows, where_ref, mine_ref, other_ref, sparse_ref, kept_ref, sent_ref, left_ref):
    row, col = where_ref[0], where_ref[1]
    core = col % 2
    sign = 1 - 2 * core
    piece = left_ref.shape[0] // rows
    half = rows // 2
    order = [t for start in (0, 2, 1, 3) for t in range(start, rows, 4)]
    for place, t in enumerate(order):
        target = (row + sign * t + rows) % rows
        source = pl.ds(pl.multiple_of((target % half) * piece, piece), piece)
        spot = pl.ds(place * piece, piece)

        @pl.when(target // half == core)
        def _():
            left_ref[spot, :] = mine_ref[source, :]

        @pl.when(target // half != core)
        def _():
            left_ref[spot, :] = other_ref[source, :]

    three = jnp.where(row == col, 3.0, 0.0).astype(F32)
    tile = min(256, sparse_ref.shape[1])
    middle = left_ref.shape[0] // 2
    for n in range(0, sparse_ref.shape[1], tile):
        spot = pl.ds(n, tile)
        product = jnp.dot(left_ref[...], sparse_ref[:, spot], preferred_element_type=F32)
        total = three * left_ref[:, spot].astype(F32) - 2.0 * product
        kept_ref[:, spot] = total[:middle]
        sent_ref[:, spot] = total[middle:].astype(BF16)


def order_kernel(groups, where_ref, kept_ref, got_ref, out_ref):
    row, col = where_ref[0], where_ref[1]
    sign = 1 - 2 * (col % 2)
    piece = out_ref.shape[0] // groups
    for u in range(groups):
        place = (row // 4 + sign * u + groups) % groups
        source = pl.ds(u * piece, piece)
        total = kept_ref[source, :] + got_ref[source, :].astype(F32)
        out_ref[pl.ds(pl.multiple_of(place * piece, piece), piece), :] = total.astype(BF16)


def body(rows, cols, density, occupancy, product_keep):
    rows_here, cols_here = density.shape
    window = product_keep.shape[0] * BS
    row, col = lax.axis_index("row"), lax.axis_index("col")
    where = jnp.stack([row, col]).astype(jnp.int32)
    half = window // 2
    piece = window // rows
    chips = cols // 2
    tall = jax.ShapeDtypeStruct

    def pairs(step, every):
        return [
            (z * cols + c, ((z + (step if c % 2 == 0 else -step)) % rows) * cols + c)
            for z in range(0, rows, every)
            for c in range(cols)
        ]

    swap = [(c, c ^ 1) for c in range(cols)]
    same_core = [[2 * i + k for i in range(chips)] for k in range(2)]
    groups = rows // 4
    strided = [[4 * i + o for i in range(groups)] for o in range(4)]

    def mask(across, down_first, across_first):
        kept = lax.dynamic_slice(product_keep, (down_first, across_first), (1, across))
        return jnp.repeat(kept, BS, axis=1).astype(F32)

    sparse, panel = call(
        mask_kernel, (tall(density.shape, BF16), tall((window, cols_here), BF16)), 10**6
    )(in_specs=[SMEM, SMEM, VMEM])(where, occupancy, density)

    halves = [panel[:half], panel[half:]]
    step = rows // 2
    while step:
        halves = [h + lax.ppermute(h, BOTH, pairs(step, 2 * step)) for h in halves]
        step //= 2

    kept, sent = call(
        square_kernel, (tall((half, rows_here), F32), tall((half, rows_here), BF16)), 2 * window * rows_here * cols_here
    )(in_specs=[SMEM, VMEM, VMEM, VMEM])(where, *halves, sparse)
    kept = (kept + lax.ppermute(sent, "col", swap).astype(F32)).astype(BF16)
    parts = lax.all_to_all(kept.reshape(chips, piece, rows_here), "col", 0, 0, axis_index_groups=same_core, tiled=True)
    first = (col % 2) * half + (col // 2) * piece
    square = parts.astype(F32).sum(0) * mask(rows_here // BS, first // BS, row * (rows_here // BS))
    square = jnp.broadcast_to(square.astype(BF16), (chips, piece, rows_here))
    mine = lax.all_to_all(square, "col", 0, 0, axis_index_groups=same_core, tiled=True).reshape(half, rows_here)
    other = lax.ppermute(mine, "col", swap)

    kept, sent = call(
        functools.partial(cube_kernel, rows),
        (tall((half, cols_here), F32), tall((half, cols_here), BF16)),
        2 * window * rows_here * cols_here,
        [pltpu.VMEM((window, rows_here), BF16)],
    )(in_specs=[SMEM, VMEM, VMEM, VMEM])(where, mine, other, sparse)
    kept = kept + lax.ppermute(sent, BOTH, pairs(1, 1)).astype(F32)
    quarter = half // 2
    got = lax.ppermute(kept[quarter:].astype(BF16), BOTH, pairs(2, 1))
    ready = call(functools.partial(order_kernel, groups), tall((quarter, cols_here), BF16), 10**6)(
        in_specs=[SMEM, VMEM, VMEM]
    )(where, kept[:quarter], got)
    parts = lax.all_to_all(ready.reshape(groups, piece, cols_here), "row", 0, 0, axis_index_groups=strided, tiled=True)
    result = parts.astype(F32).sum(0)
    result = result * mask(cols_here // BS, row * piece // BS, col * (cols_here // BS))
    return result.astype(BF16)


def solution(mesh):
    rows, cols = mesh.shape["row"], mesh.shape["col"]
    return jax.shard_map(
        functools.partial(body, rows, cols),
        mesh=mesh,
        in_specs=(P("row", "col"), P("row", "col"), P()),
        out_specs=P("row", "col"),
        check_vma=False,
    )
```

```python
import functools

import jax
import jax.numpy as jnp
from jax import lax
from jax.experimental import pallas as pl
from jax.experimental.pallas import tpu as pltpu
from jax.sharding import PartitionSpec as P

BS = 128
BF16 = jnp.bfloat16
F32 = jnp.float32
VMEM = pl.BlockSpec(memory_space=pltpu.VMEM)
SMEM = pl.BlockSpec(memory_space=pltpu.SMEM)
BOTH = ("row", "col")


def call(kernel, outs, cost, scratch=()):
    return functools.partial(
        pl.pallas_call,
        kernel,
        out_shape=outs,
        out_specs=jax.tree.map(lambda _: VMEM, outs),
        scratch_shapes=list(scratch),
        compiler_params=pltpu.CompilerParams(vmem_limit_bytes=24 * 2**20),
        cost_estimate=pl.CostEstimate(flops=cost, bytes_accessed=4 * 2**20, transcendentals=0),
    )


def panel_kernel(where_ref, occ_ref, density_ref, *half_refs):
    first = where_ref[0] == 0
    blocks = half_refs[0].shape[0] // BS
    for i in range(2 * blocks):
        for j in range(occ_ref.shape[1]):
            across = pl.ds(j * BS, BS)
            kept = density_ref[pl.ds(i * BS, BS), across] * occ_ref[i, j].astype(F32).astype(BF16)
            half_refs[i // blocks][pl.ds(i % blocks * BS, BS), across] = jnp.where(first, kept, jnp.zeros_like(kept))


def mask_kernel(occ_ref, density_ref, sparse_ref):
    for i in range(occ_ref.shape[0]):
        for j in range(occ_ref.shape[1]):
            spot = (pl.ds(i * BS, BS), pl.ds(j * BS, BS))
            sparse_ref[spot] = density_ref[spot] * occ_ref[i, j].astype(F32).astype(BF16)


def square_part(left_ref, sparse_ref, n):
    return lax.dot_general(
        left_ref[...], sparse_ref[n, :], (((1,), (1,)), ((), ())), preferred_element_type=F32
    )


def tiles(size):
    tile = min(256, size)
    return [pl.ds(n, tile) for n in range(0, size, tile)]


def sent_kernel(where_ref, low_ref, high_ref, sparse_ref, sent_ref):
    core = where_ref[1] % 2
    for mine, left_ref in ((1, low_ref), (0, high_ref)):

        @pl.when(core == mine)
        def _():
            for n in tiles(sparse_ref.shape[0]):
                sent_ref[:, n] = square_part(left_ref, sparse_ref, n).astype(BF16)


def kept_kernel(where_ref, low_ref, high_ref, sparse_ref, got_ref, kept_ref):
    core = where_ref[1] % 2
    for mine, left_ref in ((0, low_ref), (1, high_ref)):

        @pl.when(core == mine)
        def _():
            for n in tiles(sparse_ref.shape[0]):
                total = square_part(left_ref, sparse_ref, n) + got_ref[:, n].astype(F32)
                kept_ref[:, n] = total.astype(BF16)


def cube_part(where_ref, left_ref, sparse_ref, first, kept_ref, sent_ref):
    three = jnp.where(where_ref[0] == where_ref[1], 3.0, 0.0).astype(F32)
    middle = left_ref.shape[0] // 2
    for n in tiles(kept_ref.shape[1]):
        there = pl.ds(first + n.start, n.size)
        product = jnp.dot(left_ref[...], sparse_ref[:, there], preferred_element_type=F32)
        total = three * left_ref[:, there].astype(F32) - 2.0 * product
        kept_ref[:, n] = total[:middle]
        sent_ref[:, n] = total[middle:].astype(BF16)


def first_kernel(rows, where_ref, mine_ref, other_ref, sparse_ref, left_ref, kept_ref, sent_ref):
    row, core = where_ref[0], where_ref[1] % 2
    sign = 1 - 2 * core
    piece = left_ref.shape[0] // rows
    half = rows // 2
    order = [t for start in (0, 2, 1, 3) for t in range(start, rows, 4)]
    for place, t in enumerate(order):
        target = (row + sign * t + rows) % rows
        source = pl.ds(pl.multiple_of((target % half) * piece, piece), piece)
        spot = pl.ds(place * piece, piece)
        left_ref[spot, :] = jnp.where(target // half == core, mine_ref[source, :], other_ref[source, :])
    cube_part(where_ref, left_ref, sparse_ref, 0, kept_ref, sent_ref)


def second_kernel(where_ref, left_ref, sparse_ref, kept_ref, sent_ref):
    cube_part(where_ref, left_ref, sparse_ref, kept_ref.shape[1], kept_ref, sent_ref)


def order_kernel(groups, where_ref, *refs):
    out_ref = refs[-1]
    row, col = where_ref[0], where_ref[1]
    sign = 1 - 2 * (col % 2)
    piece = out_ref.shape[0] // groups
    wide = out_ref.shape[1] // 2
    for u in range(groups):
        place = (row // 4 + sign * u + groups) % groups
        source = pl.ds(u * piece, piece)
        spot = pl.ds(pl.multiple_of(place * piece, piece), piece)
        for side in range(2):
            kept_ref, got_ref = refs[2 * side : 2 * side + 2]
            total = kept_ref[source, :] + got_ref[source, :].astype(F32)
            out_ref[spot, pl.ds(side * wide, wide)] = total.astype(BF16)


def body(rows, cols, density, occupancy, product_keep):
    rows_here, cols_here = density.shape
    window = product_keep.shape[0] * BS
    row, col = lax.axis_index("row"), lax.axis_index("col")
    where = jnp.stack([row, col]).astype(jnp.int32)
    half = window // 2
    quarter = window // 4
    piece = window // rows
    chips = cols // 2
    wide = cols_here // 2
    tall = jax.ShapeDtypeStruct
    work = window * rows_here * cols_here

    def pairs(moves):
        return [
            (z * sign % rows * cols + c, (z + step) * sign % rows * cols + c)
            for z, step in moves
            for c in range(cols)
            for sign in [1 - 2 * (c % 2)]
        ]

    swap = [(c, c ^ 1) for c in range(cols)]
    same_core = [[2 * i + k for i in range(chips)] for k in range(2)]
    groups = rows // 4
    strided = [[4 * i + o for i in range(groups)] for o in range(4)]

    def mask(across, down_first, across_first):
        kept = lax.dynamic_slice(product_keep, (down_first, across_first), (1, across))
        return jnp.repeat(kept, BS, axis=1).astype(F32)

    halves = call(panel_kernel, [tall((half, cols_here), BF16)] * 2, 10**6)(in_specs=[SMEM, SMEM, VMEM])(
        where, occupancy, density[:window]
    )
    sparse = call(mask_kernel, tall(density.shape, BF16), 10**6)(in_specs=[SMEM, VMEM])(occupancy, density)

    have, gap, stages = [0], rows, []
    while gap > 2:
        gap //= 4
        stages.append([(z, gap) for z in have])
        stages.append([(z, -gap) for z in have] + [(z + gap, gap) for z in have])
        have = [z + step * gap for z in have for step in (-1, 0, 1, 2)]
    stages.append([(z, 1) for z in have])
    for moves in stages:
        halves = [h + lax.ppermute(h, BOTH, pairs(moves)) for h in halves]

    sent = call(sent_kernel, tall((half, rows_here), BF16), work)(in_specs=[SMEM, VMEM, VMEM, VMEM])(
        where, *halves, sparse
    )
    got = lax.ppermute(sent, "col", swap)
    kept = call(kept_kernel, tall((half, rows_here), BF16), work)(in_specs=[SMEM, VMEM, VMEM, VMEM, VMEM])(
        where, *halves, sparse, got
    )
    parts = lax.all_to_all(kept.reshape(chips, piece, rows_here), "col", 0, 0, axis_index_groups=same_core, tiled=True)
    first = (col % 2) * half + (col // 2) * piece
    square = parts.astype(F32).sum(0) * mask(rows_here // BS, first // BS, row * (rows_here // BS))
    square = jnp.broadcast_to(square.astype(BF16), (chips, piece, rows_here))
    mine = lax.all_to_all(square, "col", 0, 0, axis_index_groups=same_core, tiled=True).reshape(half, rows_here)
    other = lax.ppermute(mine, "col", swap)

    pair = (tall((half, wide), F32), tall((half, wide), BF16))
    left, *first_side = call(
        functools.partial(first_kernel, rows), (tall((window, rows_here), BF16), *pair), work
    )(in_specs=[SMEM, VMEM, VMEM, VMEM])(where, mine, other, sparse)
    second_side = call(second_kernel, pair, work)(in_specs=[SMEM, VMEM, VMEM])(where, left, sparse)
    terms = []
    for kept, sent in (first_side, second_side):
        kept = kept + lax.ppermute(sent, BOTH, pairs([(z, 1) for z in range(rows)])).astype(F32)
        got = lax.ppermute(kept[quarter:].astype(BF16), BOTH, pairs([(z, 2) for z in range(rows)]))
        terms += [kept, got]
    ready = call(functools.partial(order_kernel, groups), tall((quarter, cols_here), BF16), 10**6)(
        in_specs=[SMEM] + [VMEM] * 4
    )(where, *terms)
    parts = lax.all_to_all(ready.reshape(groups, piece, cols_here), "row", 0, 0, axis_index_groups=strided, tiled=True)
    result = parts.astype(F32).sum(0)
    result = result * mask(cols_here // BS, row * piece // BS, col * (cols_here // BS))
    return result.astype(BF16)


def solution(mesh):
    rows, cols = mesh.shape["row"], mesh.shape["col"]
    return jax.shard_map(
        functools.partial(body, rows, cols),
        mesh=mesh,
        in_specs=(P("row", "col"), P("row", "col"), P()),
        out_specs=P("row", "col"),
        check_vma=False,
    )
```

```python
import functools

import jax
import jax.numpy as jnp
from jax import lax
from jax.experimental import pallas as pl
from jax.experimental.pallas import tpu as pltpu
from jax.sharding import PartitionSpec as P

BS = 128
BF16 = jnp.bfloat16
F32 = jnp.float32
VMEM = pl.BlockSpec(memory_space=pltpu.VMEM)
SMEM = pl.BlockSpec(memory_space=pltpu.SMEM)
BOTH = ("row", "col")
STEPS = (2, 1, -1, 0)


def call(kernel, outs, cost, scratch=()):
    return functools.partial(
        pl.pallas_call,
        kernel,
        out_shape=outs,
        out_specs=jax.tree.map(lambda _: VMEM, outs),
        scratch_shapes=list(scratch),
        compiler_params=pltpu.CompilerParams(vmem_limit_bytes=24 * 2**20),
        cost_estimate=pl.CostEstimate(flops=cost, bytes_accessed=4 * 2**20, transcendentals=0),
    )


def panel_kernel(where_ref, occ_ref, density_ref, mine_ref, sent_ref):
    first = where_ref[0] == 0
    core = where_ref[1] % 2
    blocks = mine_ref.shape[0] // BS
    for half, out_ref in ((core, mine_ref), (1 - core, sent_ref)):
        for i in range(blocks):
            down = half * blocks + i
            rows = pl.ds(pl.multiple_of(down * BS, BS), BS)
            for j in range(occ_ref.shape[1]):
                across = pl.ds(j * BS, BS)
                kept = density_ref[rows, across] * occ_ref[down, j].astype(F32).astype(BF16)
                out_ref[pl.ds(i * BS, BS), across] = jnp.where(first, kept, jnp.zeros_like(kept))


def mask_kernel(occ_ref, density_ref, sparse_ref):
    for i in range(occ_ref.shape[0]):
        for j in range(occ_ref.shape[1]):
            spot = (pl.ds(i * BS, BS), pl.ds(j * BS, BS))
            sparse_ref[spot] = density_ref[spot] * occ_ref[i, j].astype(F32).astype(BF16)


def square_part(left_ref, sparse_ref, n):
    return lax.dot_general(
        left_ref[...], sparse_ref[n, :], (((1,), (1,)), ((), ())), preferred_element_type=F32
    )


def tiles(size):
    tile = min(256, size)
    return [pl.ds(n, tile) for n in range(0, size, tile)]


def own_kernel(left_ref, sparse_ref, total_ref):
    for n in tiles(sparse_ref.shape[0]):
        total_ref[:, n] = square_part(left_ref, sparse_ref, n)


def both_kernel(left_ref, sparse_ref, total_ref, out_ref):
    for n in tiles(sparse_ref.shape[0]):
        out_ref[:, n] = (total_ref[:, n] + square_part(left_ref, sparse_ref, n)).astype(BF16)


def cube_part(where_ref, left_ref, sparse_ref, first, low_ref, high_ref):
    three = jnp.where(where_ref[0] == where_ref[1], 3.0, 0.0).astype(F32)
    size = low_ref.shape[0]
    rows = pl.ds(first, 2 * size)
    for n in tiles(low_ref.shape[1]):
        product = jnp.dot(left_ref[rows, :], sparse_ref[:, n], preferred_element_type=F32)
        total = three * left_ref[rows, n].astype(F32) - 2.0 * product
        low_ref[:, n] = total[:size].astype(low_ref.dtype)
        high_ref[:, n] = total[size:].astype(high_ref.dtype)


def first_kernel(rows, where_ref, mine_ref, other_ref, sparse_ref, left_ref, low_ref, high_ref):
    row, core = where_ref[0], where_ref[1] % 2
    sign = 1 - 2 * core
    piece = left_ref.shape[0] // rows
    half = rows // 2
    order = [(t + rows) % rows for start in STEPS for t in range(start, start + rows, 4)]
    for place, t in enumerate(order):
        target = (row + sign * t + rows) % rows
        source = pl.ds(pl.multiple_of((target % half) * piece, piece), piece)
        spot = pl.ds(place * piece, piece)
        left_ref[spot, :] = jnp.where(target // half == core, mine_ref[source, :], other_ref[source, :])
    cube_part(where_ref, left_ref, sparse_ref, 0, low_ref, high_ref)


def second_kernel(where_ref, left_ref, sparse_ref, low_ref, high_ref):
    cube_part(where_ref, left_ref, sparse_ref, 2 * low_ref.shape[0], low_ref, high_ref)


def order_kernel(groups, where_ref, kept_ref, *refs):
    *got_refs, out_ref = refs
    row, col = where_ref[0], where_ref[1]
    sign = 1 - 2 * (col % 2)
    piece = out_ref.shape[0] // groups
    for u in range(groups):
        place = (row // 4 + sign * u + groups) % groups
        source = pl.ds(u * piece, piece)
        total = kept_ref[source, :]
        for got_ref in got_refs:
            total += got_ref[source, :].astype(F32)
        out_ref[pl.ds(pl.multiple_of(place * piece, piece), piece), :] = total.astype(BF16)


def body(rows, cols, density, occupancy, product_keep):
    rows_here, cols_here = density.shape
    window = product_keep.shape[0] * BS
    row, col = lax.axis_index("row"), lax.axis_index("col")
    where = jnp.stack([row, col]).astype(jnp.int32)
    half = window // 2
    piece = window // rows
    chips = cols // 2
    tall = jax.ShapeDtypeStruct
    work = window * rows_here * cols_here

    def pairs(moves):
        return [
            (z * sign % rows * cols + c, (z + step) * sign % rows * cols + c)
            for z, step in moves
            for c in range(cols)
            for sign in [1 - 2 * (c % 2)]
        ]

    same_core = [[2 * i + k for i in range(chips)] for k in range(2)]
    groups = rows // 4
    strided = [[4 * i + o for i in range(groups)] for o in range(4)]

    def mask(across, down_first, across_first):
        kept = lax.dynamic_slice(product_keep, (down_first, across_first), (1, across))
        return jnp.repeat(kept, BS, axis=1).astype(F32)

    swap = [(c, c ^ 1) for c in range(cols)]
    mine, sent = call(panel_kernel, [tall((half, cols_here), BF16)] * 2, 10**6)(in_specs=[SMEM, SMEM, VMEM])(
        where, occupancy, density[:window]
    )
    halves = [mine, lax.ppermute(sent, BOTH, swap)]
    sparse = call(mask_kernel, tall(density.shape, BF16), 10**6)(in_specs=[SMEM, VMEM])(occupancy, density)
    sibling = lax.ppermute(sparse, "col", swap)

    have, gap, stages = [0], rows, []
    while gap > 2:
        gap //= 4
        stages.append([(z, gap) for z in have])
        stages.append([(z, -gap) for z in have] + [(z + gap, gap) for z in have])
        have = [z + step * gap for z in have for step in (-1, 0, 1, 2)]
    stages.append([(z, 1) for z in have])
    for moves in stages:
        halves = [h + lax.ppermute(h, BOTH, pairs(moves)) for h in halves]

    total = call(own_kernel, tall((half, rows_here), F32), work)(in_specs=[VMEM] * 2)(halves[0], sparse)
    kept = call(both_kernel, tall((half, rows_here), BF16), work)(in_specs=[VMEM] * 3)(halves[1], sibling, total)
    parts = lax.all_to_all(kept.reshape(chips, piece, rows_here), "col", 0, 0, axis_index_groups=same_core, tiled=True)
    first = (col % 2) * half + (col // 2) * piece
    square = parts.astype(F32).sum(0) * mask(rows_here // BS, first // BS, row * (rows_here // BS))
    square = jnp.broadcast_to(square.astype(BF16), (chips, piece, rows_here))
    mine = lax.all_to_all(square, "col", 0, 0, axis_index_groups=same_core, tiled=True).reshape(half, rows_here)
    other = lax.ppermute(mine, "col", swap)

    quarter = tall((window // 4, cols_here), BF16)
    left, *sent = call(
        functools.partial(first_kernel, rows), (tall((window, rows_here), BF16), quarter, quarter), work
    )(in_specs=[SMEM, VMEM, VMEM, VMEM])(where, mine, other, sparse)
    last, kept = call(second_kernel, (quarter, tall(quarter.shape, F32)), work)(in_specs=[SMEM, VMEM, VMEM])(
        where, left, sparse
    )
    got = [
        lax.ppermute(part, BOTH, pairs([(z, step) for z in range(rows)]))
        for part, step in zip((*sent, last), STEPS)
    ]
    ready = call(functools.partial(order_kernel, groups), quarter, 10**6)(in_specs=[SMEM] + [VMEM] * 4)(
        where, kept, *got
    )
    parts = lax.all_to_all(ready.reshape(groups, piece, cols_here), "row", 0, 0, axis_index_groups=strided, tiled=True)
    result = parts.astype(F32).sum(0)
    result = result * mask(cols_here // BS, row * piece // BS, col * (cols_here // BS))
    return result.astype(BF16)


def solution(mesh):
    rows, cols = mesh.shape["row"], mesh.shape["col"]
    return jax.shard_map(
        functools.partial(body, rows, cols),
        mesh=mesh,
        in_specs=(P("row", "col"), P("row", "col"), P()),
        out_specs=P("row", "col"),
        check_vma=False,
    )
```

```python
import functools

import jax
import jax.numpy as jnp
from jax import lax
from jax.experimental import pallas as pl
from jax.experimental.pallas import tpu as pltpu
from jax.sharding import PartitionSpec as P

BS = 128
BF16 = jnp.bfloat16
F32 = jnp.float32
VMEM = pl.BlockSpec(memory_space=pltpu.VMEM)
SMEM = pl.BlockSpec(memory_space=pltpu.SMEM)
BOTH = ("row", "col")
STEPS = (2, 1, -1, 0)


def call(kernel, outs, cost):
    return functools.partial(
        pl.pallas_call,
        kernel,
        out_shape=outs,
        out_specs=jax.tree.map(lambda _: VMEM, outs),
        compiler_params=pltpu.CompilerParams(vmem_limit_bytes=24 * 2**20),
        cost_estimate=pl.CostEstimate(flops=cost, bytes_accessed=4 * 2**20, transcendentals=0),
    )


def panel_kernel(where_ref, occ_ref, window_ref, mine_ref, sent_ref):
    core = where_ref[1] % 2
    blocks = mine_ref.shape[0] // BS

    @pl.when(where_ref[0] != 0)
    def _():
        mine_ref[...] = jnp.zeros_like(mine_ref)
        sent_ref[...] = jnp.zeros_like(sent_ref)

    @pl.when(where_ref[0] == 0)
    def _():
        for half, out_ref in ((core, mine_ref), (1 - core, sent_ref)):
            for i in range(blocks):
                down = half * blocks + i
                rows = pl.ds(pl.multiple_of(down * BS, BS), BS)
                for j in range(occ_ref.shape[1]):
                    across = pl.ds(j * BS, BS)
                    kept = window_ref[rows, across] * occ_ref[down, j].astype(F32).astype(BF16)
                    out_ref[pl.ds(i * BS, BS), across] = kept


def mask_kernel(occ_ref, density_ref, sparse_ref):
    for i in range(occ_ref.shape[0]):
        for j in range(occ_ref.shape[1]):
            spot = (pl.ds(i * BS, BS), pl.ds(j * BS, BS))
            sparse_ref[spot] = density_ref[spot] * occ_ref[i, j].astype(F32).astype(BF16)


def square_part(left_ref, sparse_ref, n):
    return lax.dot_general(
        left_ref[...], sparse_ref[n, :], (((1,), (1,)), ((), ())), preferred_element_type=F32
    )


def tiles(size):
    tile = min(256, size)
    return [pl.ds(n, tile) for n in range(0, size, tile)]


def own_kernel(left_ref, sparse_ref, total_ref):
    for n in tiles(sparse_ref.shape[0]):
        total_ref[:, n] = square_part(left_ref, sparse_ref, n)


def both_kernel(left_ref, sparse_ref, total_ref, out_ref):
    for n in tiles(sparse_ref.shape[0]):
        out_ref[:, n] = (total_ref[:, n] + square_part(left_ref, sparse_ref, n)).astype(BF16)


def cube_part(where_ref, left_ref, sparse_ref, first, low_ref, high_ref):
    three = jnp.where(where_ref[0] == where_ref[1], 3.0, 0.0).astype(F32)
    size = low_ref.shape[0]
    rows = pl.ds(first, 2 * size)
    for n in tiles(low_ref.shape[1]):
        product = jnp.dot(left_ref[rows, :], sparse_ref[:, n], preferred_element_type=F32)
        total = three * left_ref[rows, n].astype(F32) - 2.0 * product
        low_ref[:, n] = total[:size].astype(low_ref.dtype)
        high_ref[:, n] = total[size:].astype(high_ref.dtype)


def first_kernel(rows, where_ref, mine_ref, other_ref, sparse_ref, left_ref, low_ref, high_ref):
    row, core = where_ref[0], where_ref[1] % 2
    sign = 1 - 2 * core
    piece = left_ref.shape[0] // rows
    half = rows // 2
    order = [(t + rows) % rows for start in STEPS for t in range(start, start + rows, 4)]
    for place, t in enumerate(order):
        target = (row + sign * t + rows) % rows
        source = pl.ds(pl.multiple_of((target % half) * piece, piece), piece)
        spot = pl.ds(place * piece, piece)
        left_ref[spot, :] = jnp.where(target // half == core, mine_ref[source, :], other_ref[source, :])
    cube_part(where_ref, left_ref, sparse_ref, 0, low_ref, high_ref)


def second_kernel(where_ref, left_ref, sparse_ref, low_ref, high_ref):
    cube_part(where_ref, left_ref, sparse_ref, 2 * low_ref.shape[0], low_ref, high_ref)


def spread(member, groups):
    return (member + (1 - member % 2) * (groups // 2)) % groups if groups % 4 == 0 else member


def order_kernel(groups, where_ref, kept_ref, *refs):
    *got_refs, out_ref = refs
    row, col = where_ref[0], where_ref[1]
    sign = 1 - 2 * (col % 2)
    piece = out_ref.shape[0] // groups
    for u in range(groups):
        place = spread((row // 4 + sign * u + groups) % groups, groups)
        source = pl.ds(u * piece, piece)
        total = kept_ref[source, :]
        for got_ref in got_refs:
            total += got_ref[source, :].astype(F32)
        out_ref[pl.ds(pl.multiple_of(place * piece, piece), piece), :] = total.astype(BF16)


def body(rows, cols, density, occupancy, product_keep):
    rows_here, cols_here = density.shape
    window = product_keep.shape[0] * BS
    row, col = lax.axis_index("row"), lax.axis_index("col")
    where = jnp.stack([row, col]).astype(jnp.int32)
    half = window // 2
    piece = window // rows
    chips = cols // 2
    tall = jax.ShapeDtypeStruct
    work = window * rows_here * cols_here

    def pairs(moves, way=1):
        return [
            (z * sign % rows * cols + c, (z + step) * sign % rows * cols + c)
            for z, step in moves
            for c in range(cols)
            for sign in [way * (1 - 2 * (c % 2))]
        ]

    same_core = [[2 * i + k for i in range(chips)] for k in range(2)]
    groups = rows // 4
    members = sorted(range(groups), key=lambda i: spread(i, groups))
    strided = [[4 * i + o for i in members] for o in range(4)]

    def mask(across, down_first, across_first):
        kept = lax.dynamic_slice(product_keep, (down_first, across_first), (1, across))
        return jnp.repeat(kept, BS, axis=1).astype(F32)

    swap = [(c, c ^ 1) for c in range(cols)]
    mine, sent = call(
        panel_kernel,
        [tall((half, cols_here), BF16)] * 2,
        10**6,
    )(in_specs=[SMEM, SMEM, VMEM])(where, occupancy, density[:window])
    halves = [mine, lax.ppermute(sent, BOTH, swap)]
    sparse = call(mask_kernel, tall(density.shape, BF16), 10**6)(in_specs=[SMEM, VMEM])(occupancy, density)
    sibling = lax.ppermute(sparse, "col", swap)
    have, gap, stages = [0], rows, []
    while gap > 2:
        gap //= 4
        stages.append([(z, gap) for z in have])
        stages.append([(z, -gap) for z in have] + [(z + gap, gap) for z in have])
        have = [z + step * gap for z in have for step in (-1, 0, 1, 2)]
    stages.append([(z, 1) for z in have])
    for moves in stages:
        halves = [h + lax.ppermute(h, BOTH, pairs(moves, way)) for h, way in zip(halves, (1, -1))]

    total = call(own_kernel, tall((half, rows_here), F32), work)(in_specs=[VMEM] * 2)(halves[0], sparse)
    kept = call(both_kernel, tall((half, rows_here), BF16), work)(in_specs=[VMEM] * 3)(halves[1], sibling, total)
    parts = lax.all_to_all(kept.reshape(chips, piece, rows_here), "col", 0, 0, axis_index_groups=same_core, tiled=True)
    first = (col % 2) * half + (col // 2) * piece
    square = parts.astype(F32).sum(0) * mask(rows_here // BS, first // BS, row * (rows_here // BS))
    square = jnp.broadcast_to(square.astype(BF16), (chips, piece, rows_here))
    mine = lax.all_to_all(square, "col", 0, 0, axis_index_groups=same_core, tiled=True).reshape(half, rows_here)
    other = lax.ppermute(mine, "col", swap)

    quarter = tall((window // 4, cols_here), BF16)
    left, *sent = call(
        functools.partial(first_kernel, rows), (tall((window, rows_here), BF16), quarter, quarter), work
    )(in_specs=[SMEM, VMEM, VMEM, VMEM])(where, mine, other, sparse)
    last, kept = call(second_kernel, (quarter, tall(quarter.shape, F32)), work)(in_specs=[SMEM, VMEM, VMEM])(
        where, left, sparse
    )
    got = [
        lax.ppermute(part, BOTH, pairs([(z, step) for z in range(rows)]))
        for part, step in zip((*sent, last), STEPS)
    ]
    ready = call(functools.partial(order_kernel, groups), quarter, 10**6)(in_specs=[SMEM] + [VMEM] * 4)(
        where, kept, *got
    )
    parts = lax.all_to_all(ready.reshape(groups, piece, cols_here), "row", 0, 0, axis_index_groups=strided, tiled=True)
    result = parts.astype(F32).sum(0)
    result = result * mask(cols_here // BS, row * piece // BS, col * (cols_here // BS))
    return result.astype(BF16)


def solution(mesh):
    rows, cols = mesh.shape["row"], mesh.shape["col"]
    return jax.shard_map(
        functools.partial(body, rows, cols),
        mesh=mesh,
        in_specs=(P("row", "col"), P("row", "col"), P()),
        out_specs=P("row", "col"),
        check_vma=False,
    )
```

```python
import functools

import jax
import jax.numpy as jnp
from jax import lax
from jax.experimental import pallas as pl
from jax.experimental.pallas import tpu as pltpu
from jax.sharding import PartitionSpec as P

BS = 128
BF16 = jnp.bfloat16
F32 = jnp.float32
VMEM = pl.BlockSpec(memory_space=pltpu.VMEM)
SMEM = pl.BlockSpec(memory_space=pltpu.SMEM)
BOTH = ("row", "col")
STEPS = (2, 1, -1, 0)


def call(kernel, outs, cost):
    return functools.partial(
        pl.pallas_call,
        kernel,
        out_shape=outs,
        out_specs=jax.tree.map(lambda _: VMEM, outs),
        compiler_params=pltpu.CompilerParams(vmem_limit_bytes=24 * 2**20),
        cost_estimate=pl.CostEstimate(flops=cost, bytes_accessed=4 * 2**20, transcendentals=0),
    )


def panel_kernel(where_ref, occ_ref, window_ref, mine_ref, sent_ref):
    core = where_ref[1] % 2
    blocks = mine_ref.shape[0] // BS

    @pl.when(where_ref[0] != 0)
    def _():
        mine_ref[...] = jnp.zeros_like(mine_ref)
        sent_ref[...] = jnp.zeros_like(sent_ref)

    @pl.when(where_ref[0] == 0)
    def _():
        for half, out_ref in ((core, mine_ref), (1 - core, sent_ref)):
            for i in range(blocks):
                down = half * blocks + i
                rows = pl.ds(pl.multiple_of(down * BS, BS), BS)
                for j in range(occ_ref.shape[1]):
                    across = pl.ds(j * BS, BS)
                    kept = window_ref[rows, across] * occ_ref[down, j].astype(F32).astype(BF16)
                    out_ref[pl.ds(i * BS, BS), across] = kept


def mask_kernel(occ_ref, density_ref, sparse_ref):
    for i in range(occ_ref.shape[0]):
        for j in range(occ_ref.shape[1]):
            spot = (pl.ds(i * BS, BS), pl.ds(j * BS, BS))
            sparse_ref[spot] = density_ref[spot] * occ_ref[i, j].astype(F32).astype(BF16)


def square_part(left_ref, sparse_ref, n):
    return lax.dot_general(
        left_ref[...], sparse_ref[n, :], (((1,), (1,)), ((), ())), preferred_element_type=F32
    )


def tiles(size):
    tile = min(256, size)
    return [pl.ds(n, tile) for n in range(0, size, tile)]


def own_kernel(left_ref, sparse_ref, total_ref):
    for n in tiles(sparse_ref.shape[0]):
        total_ref[:, n] = square_part(left_ref, sparse_ref, n)


def both_kernel(left_ref, sparse_ref, total_ref, out_ref):
    for n in tiles(sparse_ref.shape[0]):
        out_ref[:, n] = (total_ref[:, n] + square_part(left_ref, sparse_ref, n)).astype(BF16)


def cube_part(where_ref, left_ref, sparse_ref, first, low_ref, high_ref):
    three = jnp.where(where_ref[0] == where_ref[1], 3.0, 0.0).astype(F32)
    size = low_ref.shape[0]
    rows = pl.ds(first, 2 * size)
    for n in tiles(low_ref.shape[1]):
        product = jnp.dot(left_ref[rows, :], sparse_ref[:, n], preferred_element_type=F32)
        total = three * left_ref[rows, n].astype(F32) - 2.0 * product
        low_ref[:, n] = total[:size].astype(low_ref.dtype)
        high_ref[:, n] = total[size:].astype(high_ref.dtype)


def first_kernel(rows, where_ref, mine_ref, other_ref, sparse_ref, left_ref, low_ref, high_ref):
    row, core = where_ref[0], where_ref[1] % 2
    sign = 1 - 2 * core
    piece = left_ref.shape[0] // rows
    half = rows // 2
    order = [(t + rows) % rows for start in STEPS for t in range(start, start + rows, 4)]
    for place, t in enumerate(order):
        target = (row + sign * t + rows) % rows
        source = pl.ds(pl.multiple_of((target % half) * piece, piece), piece)
        spot = pl.ds(place * piece, piece)
        left_ref[spot, :] = jnp.where(target // half == core, mine_ref[source, :], other_ref[source, :])
    cube_part(where_ref, left_ref, sparse_ref, 0, low_ref, high_ref)


def second_kernel(where_ref, left_ref, sparse_ref, low_ref, high_ref):
    cube_part(where_ref, left_ref, sparse_ref, 2 * low_ref.shape[0], low_ref, high_ref)


def spread(member, groups):
    return (member + (1 - member % 2) * (groups // 2)) % groups if groups % 4 == 0 else member


def order_kernel(groups, where_ref, kept_ref, *refs):
    *got_refs, out_ref = refs
    row, col = where_ref[0], where_ref[1]
    sign = 1 - 2 * (col % 2)
    piece = out_ref.shape[0] // groups
    for u in range(groups):
        place = spread((row // 4 + sign * u + groups) % groups, groups)
        source = pl.ds(u * piece, piece)
        total = kept_ref[source, :]
        for got_ref in got_refs:
            total += got_ref[source, :].astype(F32)
        out_ref[pl.ds(pl.multiple_of(place * piece, piece), piece), :] = total.astype(BF16)


def body(rows, cols, density, occupancy, product_keep):
    rows_here, cols_here = density.shape
    window = product_keep.shape[0] * BS
    row, col = lax.axis_index("row"), lax.axis_index("col")
    where = jnp.stack([row, col]).astype(jnp.int32)
    half = window // 2
    piece = window // rows
    chips = cols // 2
    tall = jax.ShapeDtypeStruct
    work = window * rows_here * cols_here

    def pairs(moves, way=1):
        return [
            (z * sign % rows * cols + c, (z + step) * sign % rows * cols + c)
            for z, step in moves
            for c in range(cols)
            for sign in [way * (1 - 2 * (c % 2))]
        ]

    same_core = [[2 * i + k for i in range(chips)] for k in range(2)]
    groups = rows // 4
    members = sorted(range(groups), key=lambda i: spread(i, groups))
    strided = [[4 * i + o for i in members] for o in range(4)]

    def mask(across, down_first, across_first):
        kept = lax.dynamic_slice(product_keep, (down_first, across_first), (1, across))
        return jnp.repeat(kept, BS, axis=1).astype(F32)

    swap = [(c, c ^ 1) for c in range(cols)]
    mine, sent = call(
        panel_kernel,
        [tall((half, cols_here), BF16)] * 2,
        10**6,
    )(in_specs=[SMEM, SMEM, VMEM])(where, occupancy, density[:window])
    halves = [mine, lax.ppermute(sent, BOTH, swap)]
    sparse = call(mask_kernel, tall(density.shape, BF16), 10**6)(in_specs=[SMEM, VMEM])(occupancy, density)
    sibling = lax.ppermute(sparse, "col", swap)
    have, gap, stages = [0], rows, []
    while gap > 2:
        gap //= 4
        stages.append([(z, gap) for z in have])
        stages.append([(z, -gap) for z in have] + [(z + gap, gap) for z in have])
        have = [z + step * gap for z in have for step in (-1, 0, 1, 2)]
    stages.append([(z, 1) for z in have])
    first = (col % 2) * half + (col // 2) * piece
    masks = (
        mask(rows_here // BS, first // BS, row * (rows_here // BS)),
        mask(cols_here // BS, row * piece // BS, col * (cols_here // BS)),
    )
    for number, moves in enumerate(stages):
        halves = [h + lax.ppermute(h, BOTH, pairs(moves, way)) for h, way in zip(halves, (1, -1))]
        if number == len(stages) - 2:
            halves[1], *masks = lax.optimization_barrier((halves[1], *masks))

    total = call(own_kernel, tall((half, rows_here), F32), work)(in_specs=[VMEM] * 2)(halves[0], sparse)
    kept = call(both_kernel, tall((half, rows_here), BF16), work)(in_specs=[VMEM] * 3)(halves[1], sibling, total)
    parts = lax.all_to_all(kept.reshape(chips, piece, rows_here), "col", 0, 0, axis_index_groups=same_core, tiled=True)
    square = parts.astype(F32).sum(0) * masks[0]
    square = jnp.broadcast_to(square.astype(BF16), (chips, piece, rows_here))
    mine = lax.all_to_all(square, "col", 0, 0, axis_index_groups=same_core, tiled=True).reshape(half, rows_here)
    other = lax.ppermute(mine, "col", swap)

    quarter = tall((window // 4, cols_here), BF16)
    left, *sent = call(
        functools.partial(first_kernel, rows), (tall((window, rows_here), BF16), quarter, quarter), work
    )(in_specs=[SMEM, VMEM, VMEM, VMEM])(where, mine, other, sparse)
    last, kept = call(second_kernel, (quarter, tall(quarter.shape, F32)), work)(in_specs=[SMEM, VMEM, VMEM])(
        where, left, sparse
    )
    got = [
        lax.ppermute(part, BOTH, pairs([(z, step) for z in range(rows)]))
        for part, step in zip((*sent, last), STEPS)
    ]
    ready = call(functools.partial(order_kernel, groups), quarter, 10**6)(in_specs=[SMEM] + [VMEM] * 4)(
        where, kept, *got
    )
    parts = lax.all_to_all(ready.reshape(groups, piece, cols_here), "row", 0, 0, axis_index_groups=strided, tiled=True)
    result = parts.astype(F32).sum(0)
    return (result * masks[1]).astype(BF16)


def solution(mesh):
    rows, cols = mesh.shape["row"], mesh.shape["col"]
    return jax.shard_map(
        functools.partial(body, rows, cols),
        mesh=mesh,
        in_specs=(P("row", "col"), P("row", "col"), P()),
        out_specs=P("row", "col"),
        check_vma=False,
    )
```

```python
import functools

import jax
import jax.numpy as jnp
from jax import lax
from jax.experimental import pallas as pl
from jax.experimental.pallas import tpu as pltpu
from jax.sharding import PartitionSpec as P

BS = 128
BF16 = jnp.bfloat16
F32 = jnp.float32
VMEM = pl.BlockSpec(memory_space=pltpu.VMEM)
SMEM = pl.BlockSpec(memory_space=pltpu.SMEM)
BOTH = ("row", "col")
STEPS = (2, 1, -1, 0)


def call(kernel, outs, cost):
    return functools.partial(
        pl.pallas_call,
        kernel,
        out_shape=outs,
        out_specs=jax.tree.map(lambda _: VMEM, outs),
        compiler_params=pltpu.CompilerParams(vmem_limit_bytes=24 * 2**20),
        cost_estimate=pl.CostEstimate(flops=cost, bytes_accessed=4 * 2**20, transcendentals=0),
    )


def panel_kernel(where_ref, occ_ref, window_ref, mine_ref, sent_ref):
    core = where_ref[1] % 2
    blocks = mine_ref.shape[0] // BS

    @pl.when(where_ref[0] != 0)
    def _():
        mine_ref[...] = jnp.zeros_like(mine_ref)
        sent_ref[...] = jnp.zeros_like(sent_ref)

    @pl.when(where_ref[0] == 0)
    def _():
        for half, out_ref in ((core, mine_ref), (1 - core, sent_ref)):
            for i in range(blocks):
                down = half * blocks + i
                rows = pl.ds(pl.multiple_of(down * BS, BS), BS)
                for j in range(occ_ref.shape[1]):
                    across = pl.ds(j * BS, BS)
                    kept = window_ref[rows, across] * occ_ref[down, j].astype(F32).astype(BF16)
                    out_ref[pl.ds(i * BS, BS), across] = kept


def mask_kernel(occ_ref, density_ref, sparse_ref):
    for i in range(occ_ref.shape[0]):
        for j in range(occ_ref.shape[1]):
            spot = (pl.ds(i * BS, BS), pl.ds(j * BS, BS))
            sparse_ref[spot] = density_ref[spot] * occ_ref[i, j].astype(F32).astype(BF16)


def square_part(left_ref, sparse_ref, n):
    return lax.dot_general(
        left_ref[...], sparse_ref[n, :], (((1,), (1,)), ((), ())), preferred_element_type=F32
    )


def tiles(size):
    tile = min(256, size)
    return [pl.ds(n, tile) for n in range(0, size, tile)]


def own_kernel(left_ref, sparse_ref, total_ref):
    for n in tiles(sparse_ref.shape[0]):
        total_ref[:, n] = square_part(left_ref, sparse_ref, n)


def both_kernel(left_ref, sparse_ref, total_ref, out_ref):
    for n in tiles(sparse_ref.shape[0]):
        out_ref[:, n] = (total_ref[:, n] + square_part(left_ref, sparse_ref, n)).astype(BF16)


def cube_part(where_ref, left_ref, sparse_ref, first, low_ref, high_ref):
    three = jnp.where(where_ref[0] == where_ref[1], 3.0, 0.0).astype(F32)
    size = low_ref.shape[0]
    rows = pl.ds(first, 2 * size)
    for n in tiles(low_ref.shape[1]):
        product = jnp.dot(left_ref[rows, :], sparse_ref[:, n], preferred_element_type=F32)
        total = three * left_ref[rows, n].astype(F32) - 2.0 * product
        low_ref[:, n] = total[:size].astype(low_ref.dtype)
        high_ref[:, n] = total[size:].astype(high_ref.dtype)


def first_kernel(rows, where_ref, mine_ref, other_ref, sparse_ref, left_ref, low_ref, high_ref):
    row, core = where_ref[0], where_ref[1] % 2
    sign = 1 - 2 * core
    piece = left_ref.shape[0] // rows
    half = rows // 2
    order = [(t + rows) % rows for start in STEPS for t in range(start, start + rows, 4)]
    for place, t in enumerate(order):
        target = (row + sign * t + rows) % rows
        source = pl.ds(pl.multiple_of((target % half) * piece, piece), piece)
        spot = pl.ds(place * piece, piece)
        left_ref[spot, :] = jnp.where(target // half == core, mine_ref[source, :], other_ref[source, :])
    cube_part(where_ref, left_ref, sparse_ref, 0, low_ref, high_ref)


def second_kernel(where_ref, left_ref, sparse_ref, low_ref, high_ref):
    cube_part(where_ref, left_ref, sparse_ref, 2 * low_ref.shape[0], low_ref, high_ref)


def spread(member, groups):
    return (member + (1 - member % 2) * (groups // 2)) % groups if groups % 4 == 0 else member


def order_kernel(groups, where_ref, kept_ref, *refs):
    *got_refs, out_ref = refs
    row, col = where_ref[0], where_ref[1]
    sign = 1 - 2 * (col % 2)
    piece = out_ref.shape[0] // groups
    for u in range(groups):
        place = spread((row // 4 + sign * u + groups) % groups, groups)
        source = pl.ds(u * piece, piece)
        total = kept_ref[source, :]
        for got_ref in got_refs:
            total += got_ref[source, :].astype(F32)
        out_ref[pl.ds(pl.multiple_of(place * piece, piece), piece), :] = total.astype(BF16)


def body(rows, cols, density, occupancy, product_keep):
    rows_here, cols_here = density.shape
    window = product_keep.shape[0] * BS
    row, col = lax.axis_index("row"), lax.axis_index("col")
    where = jnp.stack([row, col]).astype(jnp.int32)
    half = window // 2
    piece = window // rows
    chips = cols // 2
    tall = jax.ShapeDtypeStruct
    work = window * rows_here * cols_here

    def pairs(moves, ways):
        return [
            (z * sign % rows * cols + c, (z + step) * sign % rows * cols + c)
            for z, step in moves
            for c in range(cols)
            for sign in [ways[c % 2]]
        ]

    same_core = [[2 * i + k for i in range(chips)] for k in range(2)]
    groups = rows // 4
    members = sorted(range(groups), key=lambda i: spread(i, groups))
    strided = [[4 * i + o for i in members] for o in range(4)]

    def mask(across, down_first, across_first):
        kept = lax.dynamic_slice(product_keep, (down_first, across_first), (1, across))
        return jnp.repeat(kept, BS, axis=1).astype(F32)

    swap = [(c, c ^ 1) for c in range(cols)]
    mine, sent = call(
        panel_kernel,
        [tall((half, cols_here), BF16)] * 2,
        10**6,
    )(in_specs=[SMEM, SMEM, VMEM])(where, occupancy, density[:window])
    halves = [mine, lax.ppermute(sent, BOTH, swap)]
    sparse = call(mask_kernel, tall(density.shape, BF16), 10**6)(in_specs=[SMEM, VMEM])(occupancy, density)
    sibling = lax.ppermute(sparse, "col", swap)
    have, gap, stages = [0], rows, []
    while gap > 2:
        gap //= 4
        stages.append([(z, gap) for z in have])
        stages.append([(z, -gap) for z in have] + [(z + gap, gap) for z in have])
        have = [z + step * gap for z in have for step in (-1, 0, 1, 2)]
    stages.append([(z, 1) for z in have])
    for moves in stages:
        halves = [h + lax.ppermute(h, BOTH, pairs(moves, (way, way))) for h, way in zip(halves, (1, -1))]

    total = call(own_kernel, tall((half, rows_here), F32), work)(in_specs=[VMEM] * 2)(halves[0], sparse)
    kept = call(both_kernel, tall((half, rows_here), BF16), work)(in_specs=[VMEM] * 3)(halves[1], sibling, total)
    parts = lax.all_to_all(kept.reshape(chips, piece, rows_here), "col", 0, 0, axis_index_groups=same_core, tiled=True)
    first = (col % 2) * half + (col // 2) * piece
    square = parts.astype(F32).sum(0) * mask(rows_here // BS, first // BS, row * (rows_here // BS))
    square = jnp.broadcast_to(square.astype(BF16), (chips, piece, rows_here))
    mine = lax.all_to_all(square, "col", 0, 0, axis_index_groups=same_core, tiled=True).reshape(half, rows_here)
    other = lax.ppermute(mine, "col", swap)

    quarter = tall((window // 4, cols_here), BF16)
    left, *sent = call(
        functools.partial(first_kernel, rows), (tall((window, rows_here), BF16), quarter, quarter), work
    )(in_specs=[SMEM, VMEM, VMEM, VMEM])(where, mine, other, sparse)
    last, kept = call(second_kernel, (quarter, tall(quarter.shape, F32)), work)(in_specs=[SMEM, VMEM, VMEM])(
        where, left, sparse
    )
    got = [
        lax.ppermute(part, BOTH, pairs([(z, step) for z in range(rows)], (1, -1)))
        for part, step in zip((*sent, last), STEPS)
    ]
    ready = call(functools.partial(order_kernel, groups), quarter, 10**6)(in_specs=[SMEM] + [VMEM] * 4)(
        where, kept, *got
    )
    parts = lax.all_to_all(ready.reshape(groups, piece, cols_here), "row", 0, 0, axis_index_groups=strided, tiled=True)
    result = parts.astype(F32).sum(0)
    result = result * mask(cols_here // BS, row * piece // BS, col * (cols_here // BS))
    return result.astype(BF16)


def solution(mesh):
    rows, cols = mesh.shape["row"], mesh.shape["col"]
    return jax.shard_map(
        functools.partial(body, rows, cols),
        mesh=mesh,
        in_specs=(P("row", "col"), P("row", "col"), P()),
        out_specs=P("row", "col"),
        check_vma=False,
    )
```

```python
import functools

import jax
import jax.numpy as jnp
from jax import lax
from jax.experimental import pallas as pl
from jax.experimental.pallas import tpu as pltpu
from jax.sharding import PartitionSpec as P

BS = 128
BF16 = jnp.bfloat16
F32 = jnp.float32
VMEM = pl.BlockSpec(memory_space=pltpu.VMEM)
SMEM = pl.BlockSpec(memory_space=pltpu.SMEM)
BOTH = ("row", "col")
STEPS = (2, 1, -1, 0)


def call(kernel, outs, cost):
    return functools.partial(
        pl.pallas_call,
        kernel,
        out_shape=outs,
        out_specs=jax.tree.map(lambda _: VMEM, outs),
        compiler_params=pltpu.CompilerParams(vmem_limit_bytes=24 * 2**20),
        cost_estimate=pl.CostEstimate(flops=cost, bytes_accessed=4 * 2**20, transcendentals=0),
    )


def panel_kernel(where_ref, occ_ref, window_ref, mine_ref, sent_ref):
    core = where_ref[1] % 2
    blocks = mine_ref.shape[0] // BS

    @pl.when(where_ref[0] != 0)
    def _():
        mine_ref[...] = jnp.zeros_like(mine_ref)
        sent_ref[...] = jnp.zeros_like(sent_ref)

    @pl.when(where_ref[0] == 0)
    def _():
        for half, out_ref in ((core, mine_ref), (1 - core, sent_ref)):
            for i in range(blocks):
                down = half * blocks + i
                rows = pl.ds(pl.multiple_of(down * BS, BS), BS)
                for j in range(occ_ref.shape[1]):
                    across = pl.ds(j * BS, BS)
                    kept = window_ref[rows, across] * occ_ref[down, j].astype(F32).astype(BF16)
                    out_ref[pl.ds(i * BS, BS), across] = kept


def mask_kernel(occ_ref, density_ref, sparse_ref):
    for i in range(occ_ref.shape[0]):
        for j in range(occ_ref.shape[1]):
            spot = (pl.ds(i * BS, BS), pl.ds(j * BS, BS))
            sparse_ref[spot] = density_ref[spot] * occ_ref[i, j].astype(F32).astype(BF16)


def square_part(left_ref, sparse_ref, n):
    return lax.dot_general(
        left_ref[...], sparse_ref[n, :], (((1,), (1,)), ((), ())), preferred_element_type=F32
    )


def tiles(size):
    tile = min(256, size)
    return [pl.ds(n, tile) for n in range(0, size, tile)]


def own_kernel(left_ref, sparse_ref, total_ref):
    for n in tiles(sparse_ref.shape[0]):
        total_ref[:, n] = square_part(left_ref, sparse_ref, n)


def both_kernel(left_ref, sparse_ref, total_ref, out_ref):
    for n in tiles(sparse_ref.shape[0]):
        out_ref[:, n] = (total_ref[:, n] + square_part(left_ref, sparse_ref, n)).astype(BF16)


def cube_part(where_ref, left_ref, sparse_ref, first, low_ref, high_ref):
    three = jnp.where(where_ref[0] == where_ref[1], 3.0, 0.0).astype(F32)
    size = low_ref.shape[0]
    rows = pl.ds(first, 2 * size)
    for n in tiles(low_ref.shape[1]):
        product = jnp.dot(left_ref[rows, :], sparse_ref[:, n], preferred_element_type=F32)
        total = three * left_ref[rows, n].astype(F32) - 2.0 * product
        low_ref[:, n] = total[:size].astype(low_ref.dtype)
        high_ref[:, n] = total[size:].astype(high_ref.dtype)


def first_kernel(rows, where_ref, mine_ref, other_ref, sparse_ref, left_ref, low_ref, high_ref):
    row, core = where_ref[0], where_ref[1] % 2
    sign = 1 - 2 * core
    piece = left_ref.shape[0] // rows
    half = rows // 2
    order = [(t + rows) % rows for start in STEPS for t in range(start, start + rows, 4)]
    for place, t in enumerate(order):
        target = (row + sign * t + rows) % rows
        source = pl.ds(pl.multiple_of((target % half) * piece, piece), piece)
        spot = pl.ds(place * piece, piece)
        left_ref[spot, :] = jnp.where(target // half == core, mine_ref[source, :], other_ref[source, :])
    cube_part(where_ref, left_ref, sparse_ref, 0, low_ref, high_ref)


def second_kernel(where_ref, left_ref, sparse_ref, low_ref, high_ref):
    cube_part(where_ref, left_ref, sparse_ref, 2 * low_ref.shape[0], low_ref, high_ref)


def spread(member, groups):
    return (member + (1 - member % 2) * (groups // 2)) % groups if groups % 4 == 0 else member


def order_kernel(groups, where_ref, kept_ref, *refs):
    *got_refs, out_ref = refs
    row, col = where_ref[0], where_ref[1]
    sign = 1 - 2 * (col % 2)
    piece = out_ref.shape[0] // groups
    for u in range(groups):
        place = spread((row // 4 + sign * u + groups) % groups, groups)
        source = pl.ds(u * piece, piece)
        total = kept_ref[source, :]
        for got_ref in got_refs:
            total += got_ref[source, :].astype(F32)
        out_ref[pl.ds(pl.multiple_of(place * piece, piece), piece), :] = total.astype(BF16)


def body(rows, cols, density, occupancy, product_keep):
    rows_here, cols_here = density.shape
    window = product_keep.shape[0] * BS
    row, col = lax.axis_index("row"), lax.axis_index("col")
    where = jnp.stack([row, col]).astype(jnp.int32)
    half = window // 2
    piece = window // rows
    chips = cols // 2
    tall = jax.ShapeDtypeStruct
    work = window * rows_here * cols_here

    def pairs(moves, way=1):
        return [
            (z * sign % rows * cols + c, (z + step) * sign % rows * cols + c)
            for z, step in moves
            for c in range(cols)
            for sign in [way * (1 - 2 * (c % 2))]
        ]

    same_core = [[2 * i + k for i in range(chips)] for k in range(2)]
    groups = rows // 4
    members = sorted(range(groups), key=lambda i: spread(i, groups))
    strided = [[4 * i + o for i in members] for o in range(4)]

    def mask(across, down_first, across_first):
        kept = lax.dynamic_slice(product_keep, (down_first, across_first), (1, across))
        return jnp.repeat(kept, BS, axis=1).astype(F32)

    swap = [(c, c ^ 1) for c in range(cols)]
    mine, sent = call(
        panel_kernel,
        [tall((half, cols_here), BF16)] * 2,
        10**6,
    )(in_specs=[SMEM, SMEM, VMEM])(where, occupancy, density[:window])
    halves = [mine, lax.ppermute(sent, BOTH, swap)]
    sparse = call(mask_kernel, tall(density.shape, BF16), 10**6)(in_specs=[SMEM, VMEM])(occupancy, density)
    sibling = lax.ppermute(sparse, "col", swap)
    far = rows // 4
    have, gap, stages = [-far, 0, far, 2 * far], far, []
    while gap > 2:
        gap //= 4
        stages.append([(z, gap) for z in have])
        stages.append([(z, -gap) for z in have] + [(z + gap, gap) for z in have])
        have = [z + step * gap for z in have for step in (-1, 0, 1, 2)]
    stages.append([(z, 1) for z in have])
    spread_out = []
    for h, way in zip(halves, (1, -1)):
        h = h + lax.ppermute(h, BOTH, pairs([(0, far)], way)) + lax.ppermute(h, BOTH, pairs([(0, -far)], way))
        spread_out.append(h + lax.ppermute(h, BOTH, pairs([(far, far)], way)))
    halves = spread_out
    for moves in stages:
        halves = [h + lax.ppermute(h, BOTH, pairs(moves, way)) for h, way in zip(halves, (1, -1))]

    total = call(own_kernel, tall((half, rows_here), F32), work)(in_specs=[VMEM] * 2)(halves[0], sparse)
    kept = call(both_kernel, tall((half, rows_here), BF16), work)(in_specs=[VMEM] * 3)(halves[1], sibling, total)
    parts = lax.all_to_all(kept.reshape(chips, piece, rows_here), "col", 0, 0, axis_index_groups=same_core, tiled=True)
    first = (col % 2) * half + (col // 2) * piece
    square = parts.astype(F32).sum(0) * mask(rows_here // BS, first // BS, row * (rows_here // BS))
    square = jnp.broadcast_to(square.astype(BF16), (chips, piece, rows_here))
    mine = lax.all_to_all(square, "col", 0, 0, axis_index_groups=same_core, tiled=True).reshape(half, rows_here)
    other = lax.ppermute(mine, "col", swap)

    quarter = tall((window // 4, cols_here), BF16)
    left, *sent = call(
        functools.partial(first_kernel, rows), (tall((window, rows_here), BF16), quarter, quarter), work
    )(in_specs=[SMEM, VMEM, VMEM, VMEM])(where, mine, other, sparse)
    last, kept = call(second_kernel, (quarter, tall(quarter.shape, F32)), work)(in_specs=[SMEM, VMEM, VMEM])(
        where, left, sparse
    )
    got = [
        lax.ppermute(part, BOTH, pairs([(z, step) for z in range(rows)]))
        for part, step in zip((*sent, last), STEPS)
    ]
    ready = call(functools.partial(order_kernel, groups), quarter, 10**6)(in_specs=[SMEM] + [VMEM] * 4)(
        where, kept, *got
    )
    parts = lax.all_to_all(ready.reshape(groups, piece, cols_here), "row", 0, 0, axis_index_groups=strided, tiled=True)
    result = parts.astype(F32).sum(0)
    result = result * mask(cols_here // BS, row * piece // BS, col * (cols_here // BS))
    return result.astype(BF16)


def solution(mesh):
    rows, cols = mesh.shape["row"], mesh.shape["col"]
    return jax.shard_map(
        functools.partial(body, rows, cols),
        mesh=mesh,
        in_specs=(P("row", "col"), P("row", "col"), P()),
        out_specs=P("row", "col"),
        check_vma=False,
    )
```

```python
import functools

import jax
import jax.numpy as jnp
from jax import lax
from jax.experimental import pallas as pl
from jax.experimental.pallas import tpu as pltpu
from jax.sharding import PartitionSpec as P

BS = 128
BF16 = jnp.bfloat16
F32 = jnp.float32
VMEM = pl.BlockSpec(memory_space=pltpu.VMEM)
SMEM = pl.BlockSpec(memory_space=pltpu.SMEM)
BOTH = ("row", "col")
STEPS = (2, 1, -1, 0)


def call(kernel, outs, cost):
    return functools.partial(
        pl.pallas_call,
        kernel,
        out_shape=outs,
        out_specs=jax.tree.map(lambda _: VMEM, outs),
        compiler_params=pltpu.CompilerParams(vmem_limit_bytes=24 * 2**20),
        cost_estimate=pl.CostEstimate(flops=cost, bytes_accessed=4 * 2**20, transcendentals=0),
    )


def panel_kernel(where_ref, occ_ref, window_ref, mine_ref, sent_ref):
    core = where_ref[1] % 2
    blocks = mine_ref.shape[0] // BS

    @pl.when(where_ref[0] != 0)
    def _():
        mine_ref[...] = jnp.zeros_like(mine_ref)
        sent_ref[...] = jnp.zeros_like(sent_ref)

    @pl.when(where_ref[0] == 0)
    def _():
        for half, out_ref in ((core, mine_ref), (1 - core, sent_ref)):
            for i in range(blocks):
                down = half * blocks + i
                rows = pl.ds(pl.multiple_of(down * BS, BS), BS)
                for j in range(occ_ref.shape[1]):
                    across = pl.ds(j * BS, BS)
                    kept = window_ref[rows, across] * occ_ref[down, j].astype(F32).astype(BF16)
                    out_ref[pl.ds(i * BS, BS), across] = kept


def mask_kernel(occ_ref, density_ref, sparse_ref):
    for i in range(occ_ref.shape[0]):
        for j in range(occ_ref.shape[1]):
            spot = (pl.ds(i * BS, BS), pl.ds(j * BS, BS))
            sparse_ref[spot] = density_ref[spot] * occ_ref[i, j].astype(F32).astype(BF16)


def square_part(left_ref, sparse_ref, n):
    return lax.dot_general(
        left_ref[...], sparse_ref[n, :], (((1,), (1,)), ((), ())), preferred_element_type=F32
    )


def tiles(size):
    tile = min(256, size)
    return [pl.ds(n, tile) for n in range(0, size, tile)]


def own_kernel(left_ref, sparse_ref, total_ref):
    for n in tiles(sparse_ref.shape[0]):
        total_ref[:, n] = square_part(left_ref, sparse_ref, n)


def both_kernel(left_ref, sparse_ref, total_ref, out_ref):
    for n in tiles(sparse_ref.shape[0]):
        out_ref[:, n] = (total_ref[:, n] + square_part(left_ref, sparse_ref, n)).astype(BF16)


def cube_part(where_ref, left_ref, sparse_ref, first, low_ref, high_ref):
    three = jnp.where(where_ref[0] == where_ref[1], 3.0, 0.0).astype(F32)
    size = low_ref.shape[0]
    rows = pl.ds(first, 2 * size)
    for n in tiles(low_ref.shape[1]):
        product = jnp.dot(left_ref[rows, :], sparse_ref[:, n], preferred_element_type=F32)
        total = three * left_ref[rows, n].astype(F32) - 2.0 * product
        low_ref[:, n] = total[:size].astype(low_ref.dtype)
        high_ref[:, n] = total[size:].astype(high_ref.dtype)


def first_kernel(rows, where_ref, mine_ref, other_ref, sparse_ref, left_ref, low_ref, high_ref):
    row, core = where_ref[0], where_ref[1] % 2
    sign = 1 - 2 * core
    piece = left_ref.shape[0] // rows
    half = rows // 2
    order = [(t + rows) % rows for start in STEPS for t in range(start, start + rows, 4)]
    for place, t in enumerate(order):
        target = (row + sign * t + rows) % rows
        source = pl.ds(pl.multiple_of((target % half) * piece, piece), piece)
        spot = pl.ds(place * piece, piece)
        left_ref[spot, :] = jnp.where(target // half == core, mine_ref[source, :], other_ref[source, :])
    cube_part(where_ref, left_ref, sparse_ref, 0, low_ref, high_ref)


def second_kernel(where_ref, left_ref, sparse_ref, low_ref, high_ref):
    cube_part(where_ref, left_ref, sparse_ref, 2 * low_ref.shape[0], low_ref, high_ref)


def spread(member, groups):
    return (member + (1 - member % 2) * (groups // 2)) % groups if groups % 4 == 0 else member


def order_kernel(groups, where_ref, kept_ref, *refs):
    *got_refs, out_ref = refs
    row, col = where_ref[0], where_ref[1]
    sign = 1 - 2 * (col % 2)
    piece = out_ref.shape[0] // groups
    for u in range(groups):
        place = spread((row // 4 + sign * u + groups) % groups, groups)
        source = pl.ds(u * piece, piece)
        total = kept_ref[source, :]
        for got_ref in got_refs:
            total += got_ref[source, :].astype(F32)
        out_ref[pl.ds(pl.multiple_of(place * piece, piece), piece), :] = total.astype(BF16)


def body(rows, cols, density, occupancy, product_keep):
    rows_here, cols_here = density.shape
    window = product_keep.shape[0] * BS
    row, col = lax.axis_index("row"), lax.axis_index("col")
    where = jnp.stack([row, col]).astype(jnp.int32)
    half = window // 2
    piece = window // rows
    chips = cols // 2
    tall = jax.ShapeDtypeStruct
    work = window * rows_here * cols_here

    def pairs(moves, way=1):
        return [
            (z * sign % rows * cols + c, (z + step) * sign % rows * cols + c)
            for z, step in moves
            for c in range(cols)
            for sign in [way * (1 - 2 * (c % 2))]
        ]

    same_core = [[2 * i + k for i in range(chips)] for k in range(2)]
    groups = rows // 4
    members = sorted(range(groups), key=lambda i: spread(i, groups))
    strided = [[4 * i + o for i in members] for o in range(4)]

    def mask(across, down_first, across_first):
        kept = lax.dynamic_slice(product_keep, (down_first, across_first), (1, across))
        return jnp.repeat(kept, BS, axis=1).astype(F32)

    swap = [(c, c ^ 1) for c in range(cols)]
    mine, sent = call(
        panel_kernel,
        [tall((half, cols_here), BF16)] * 2,
        10**6,
    )(in_specs=[SMEM, SMEM, VMEM])(where, occupancy, density[:window])
    halves = [mine, lax.ppermute(sent, BOTH, swap)]
    sparse = call(mask_kernel, tall(density.shape, BF16), 10**6)(in_specs=[SMEM, VMEM])(occupancy, density)
    sibling = lax.ppermute(sparse, "col", swap)
    far = rows // 4
    have, gap, stages = [-far, 0, far, 2 * far], far, []
    while gap > 2:
        gap //= 4
        stages.append([(z, gap) for z in have])
        stages.append([(z, -gap) for z in have] + [(z + gap, gap) for z in have])
        have = [z + step * gap for z in have for step in (-1, 0, 1, 2)]
    stages.append([(z, 1) for z in have])
    spread_out = []
    for h, way in zip(halves, (1, -1)):
        near = h + lax.ppermute(h, BOTH, pairs([(0, far)], way))
        back = lax.ppermute(h, BOTH, pairs([(0, -far)], way))
        spread_out.append(near + back + lax.ppermute(near, BOTH, pairs([(far, far)], way)))
    halves = spread_out
    for moves in stages:
        halves = [h + lax.ppermute(h, BOTH, pairs(moves, way)) for h, way in zip(halves, (1, -1))]

    total = call(own_kernel, tall((half, rows_here), F32), work)(in_specs=[VMEM] * 2)(halves[0], sparse)
    kept = call(both_kernel, tall((half, rows_here), BF16), work)(in_specs=[VMEM] * 3)(halves[1], sibling, total)
    parts = lax.all_to_all(kept.reshape(chips, piece, rows_here), "col", 0, 0, axis_index_groups=same_core, tiled=True)
    first = (col % 2) * half + (col // 2) * piece
    square = parts.astype(F32).sum(0) * mask(rows_here // BS, first // BS, row * (rows_here // BS))
    square = jnp.broadcast_to(square.astype(BF16), (chips, piece, rows_here))
    mine = lax.all_to_all(square, "col", 0, 0, axis_index_groups=same_core, tiled=True).reshape(half, rows_here)
    other = lax.ppermute(mine, "col", swap)

    quarter = tall((window // 4, cols_here), BF16)
    left, *sent = call(
        functools.partial(first_kernel, rows), (tall((window, rows_here), BF16), quarter, quarter), work
    )(in_specs=[SMEM, VMEM, VMEM, VMEM])(where, mine, other, sparse)
    last, kept = call(second_kernel, (quarter, tall(quarter.shape, F32)), work)(in_specs=[SMEM, VMEM, VMEM])(
        where, left, sparse
    )
    got = [
        lax.ppermute(part, BOTH, pairs([(z, step) for z in range(rows)]))
        for part, step in zip((*sent, last), STEPS)
    ]
    ready = call(functools.partial(order_kernel, groups), quarter, 10**6)(in_specs=[SMEM] + [VMEM] * 4)(
        where, kept, *got
    )
    parts = lax.all_to_all(ready.reshape(groups, piece, cols_here), "row", 0, 0, axis_index_groups=strided, tiled=True)
    result = parts.astype(F32).sum(0)
    result = result * mask(cols_here // BS, row * piece // BS, col * (cols_here // BS))
    return result.astype(BF16)


def solution(mesh):
    rows, cols = mesh.shape["row"], mesh.shape["col"]
    return jax.shard_map(
        functools.partial(body, rows, cols),
        mesh=mesh,
        in_specs=(P("row", "col"), P("row", "col"), P()),
        out_specs=P("row", "col"),
        check_vma=False,
    )
```

```python
import functools

import jax
import jax.numpy as jnp
from jax import lax
from jax.experimental import pallas as pl
from jax.experimental.pallas import tpu as pltpu
from jax.sharding import PartitionSpec as P

BS = 128
BF16 = jnp.bfloat16
F32 = jnp.float32
VMEM = pl.BlockSpec(memory_space=pltpu.VMEM)
SMEM = pl.BlockSpec(memory_space=pltpu.SMEM)
BOTH = ("row", "col")
STEPS = (2, 1, -1, 0)


def call(kernel, outs, cost):
    return functools.partial(
        pl.pallas_call,
        kernel,
        out_shape=outs,
        out_specs=jax.tree.map(lambda _: VMEM, outs),
        compiler_params=pltpu.CompilerParams(vmem_limit_bytes=24 * 2**20),
        cost_estimate=pl.CostEstimate(flops=cost, bytes_accessed=4 * 2**20, transcendentals=0),
    )


def panel_kernel(where_ref, occ_ref, window_ref, mine_ref, sent_ref):
    core = where_ref[1] % 2
    blocks = mine_ref.shape[0] // BS

    @pl.when(where_ref[0] != 0)
    def _():
        mine_ref[...] = jnp.zeros_like(mine_ref)
        sent_ref[...] = jnp.zeros_like(sent_ref)

    @pl.when(where_ref[0] == 0)
    def _():
        for half, out_ref in ((core, mine_ref), (1 - core, sent_ref)):
            for i in range(blocks):
                down = half * blocks + i
                rows = pl.ds(pl.multiple_of(down * BS, BS), BS)
                for j in range(occ_ref.shape[1]):
                    across = pl.ds(j * BS, BS)
                    kept = window_ref[rows, across] * occ_ref[down, j].astype(F32).astype(BF16)
                    out_ref[pl.ds(i * BS, BS), across] = kept


def mask_kernel(occ_ref, density_ref, sparse_ref):
    for i in range(occ_ref.shape[0]):
        for j in range(occ_ref.shape[1]):
            spot = (pl.ds(i * BS, BS), pl.ds(j * BS, BS))
            sparse_ref[spot] = density_ref[spot] * occ_ref[i, j].astype(F32).astype(BF16)


def square_part(left_ref, sparse_ref, n):
    return lax.dot_general(
        left_ref[...], sparse_ref[n, :], (((1,), (1,)), ((), ())), preferred_element_type=F32
    )


def tiles(size):
    tile = min(256, size)
    return [pl.ds(n, tile) for n in range(0, size, tile)]


def own_kernel(left_ref, sparse_ref, total_ref):
    for n in tiles(sparse_ref.shape[0]):
        total_ref[:, n] = square_part(left_ref, sparse_ref, n)


def both_kernel(left_ref, sparse_ref, total_ref, out_ref):
    for n in tiles(sparse_ref.shape[0]):
        out_ref[:, n] = (total_ref[:, n] + square_part(left_ref, sparse_ref, n)).astype(BF16)


def cube_part(where_ref, left_ref, sparse_ref, first, low_ref, high_ref):
    three = jnp.where(where_ref[0] == where_ref[1], 3.0, 0.0).astype(F32)
    size = low_ref.shape[0]
    rows = pl.ds(first, 2 * size)
    for n in tiles(low_ref.shape[1]):
        product = jnp.dot(left_ref[rows, :], sparse_ref[:, n], preferred_element_type=F32)
        total = three * left_ref[rows, n].astype(F32) - 2.0 * product
        low_ref[:, n] = total[:size].astype(low_ref.dtype)
        high_ref[:, n] = total[size:].astype(high_ref.dtype)


def first_kernel(rows, where_ref, mine_ref, other_ref, sparse_ref, left_ref, low_ref, high_ref):
    row, core = where_ref[0], where_ref[1] % 2
    sign = 1 - 2 * core
    piece = left_ref.shape[0] // rows
    half = rows // 2
    order = [(t + rows) % rows for start in STEPS for t in range(start, start + rows, 4)]
    for place, t in enumerate(order):
        target = (row + sign * t + rows) % rows
        source = pl.ds(pl.multiple_of((target % half) * piece, piece), piece)
        spot = pl.ds(place * piece, piece)
        left_ref[spot, :] = jnp.where(target // half == core, mine_ref[source, :], other_ref[source, :])
    cube_part(where_ref, left_ref, sparse_ref, 0, low_ref, high_ref)


def second_kernel(where_ref, left_ref, sparse_ref, low_ref, high_ref):
    cube_part(where_ref, left_ref, sparse_ref, 2 * low_ref.shape[0], low_ref, high_ref)


def spread(member, groups):
    if groups % 4:
        return member
    away = (member + groups // 2) % groups
    return away + member % 2 * ((groups - away) % groups - away)


def order_kernel(groups, where_ref, kept_ref, *refs):
    *got_refs, out_ref = refs
    row, col = where_ref[0], where_ref[1]
    sign = 1 - 2 * (col % 2)
    piece = out_ref.shape[0] // groups
    for u in range(groups):
        place = spread((row // 4 + sign * u + groups) % groups, groups)
        source = pl.ds(u * piece, piece)
        total = kept_ref[source, :]
        for got_ref in got_refs:
            total += got_ref[source, :].astype(F32)
        out_ref[pl.ds(pl.multiple_of(place * piece, piece), piece), :] = total.astype(BF16)


def body(rows, cols, density, occupancy, product_keep):
    rows_here, cols_here = density.shape
    window = product_keep.shape[0] * BS
    row, col = lax.axis_index("row"), lax.axis_index("col")
    where = jnp.stack([row, col]).astype(jnp.int32)
    half = window // 2
    piece = window // rows
    chips = cols // 2
    tall = jax.ShapeDtypeStruct
    work = window * rows_here * cols_here

    def pairs(moves, way=1):
        return [
            (z * sign % rows * cols + c, (z + step) * sign % rows * cols + c)
            for z, step in moves
            for c in range(cols)
            for sign in [way * (1 - 2 * (c % 2))]
        ]

    same_core = [[2 * i + k for i in range(chips)] for k in range(2)]
    groups = rows // 4
    members = sorted(range(groups), key=lambda i: spread(i, groups))
    strided = [[4 * i + o for i in members] for o in range(4)]

    def mask(across, down_first, across_first):
        kept = lax.dynamic_slice(product_keep, (down_first, across_first), (1, across))
        return jnp.repeat(kept, BS, axis=1).astype(F32)

    swap = [(c, c ^ 1) for c in range(cols)]
    mine, sent = call(
        panel_kernel,
        [tall((half, cols_here), BF16)] * 2,
        10**6,
    )(in_specs=[SMEM, SMEM, VMEM])(where, occupancy, density[:window])
    halves = [mine, lax.ppermute(sent, BOTH, swap)]
    sparse = call(mask_kernel, tall(density.shape, BF16), 10**6)(in_specs=[SMEM, VMEM])(occupancy, density)
    sibling = lax.ppermute(sparse, "col", swap)
    far = rows // 4
    have, gap, stages = [-far, 0, far, 2 * far], far, []
    while gap > 2:
        gap //= 4
        stages.append([(z, gap) for z in have])
        stages.append([(z, -gap) for z in have] + [(z + gap, gap) for z in have])
        have = [z + step * gap for z in have for step in (-1, 0, 1, 2)]
    stages.append([(z, 1) for z in have])
    spread_out = []
    for h, way in zip(halves, (1, -1)):
        near = h + lax.ppermute(h, BOTH, pairs([(0, far)], way))
        back = lax.ppermute(h, BOTH, pairs([(0, -far)], way))
        spread_out.append(near + back + lax.ppermute(near, BOTH, pairs([(far, far)], way)))
    halves = spread_out
    for moves in stages:
        halves = [h + lax.ppermute(h, BOTH, pairs(moves, way)) for h, way in zip(halves, (1, -1))]

    total = call(own_kernel, tall((half, rows_here), F32), work)(in_specs=[VMEM] * 2)(halves[0], sparse)
    kept = call(both_kernel, tall((half, rows_here), BF16), work)(in_specs=[VMEM] * 3)(halves[1], sibling, total)
    parts = lax.all_to_all(kept.reshape(chips, piece, rows_here), "col", 0, 0, axis_index_groups=same_core, tiled=True)
    first = (col % 2) * half + (col // 2) * piece
    square = parts.astype(F32).sum(0) * mask(rows_here // BS, first // BS, row * (rows_here // BS))
    square = jnp.broadcast_to(square.astype(BF16), (chips, piece, rows_here))
    mine = lax.all_to_all(square, "col", 0, 0, axis_index_groups=same_core, tiled=True).reshape(half, rows_here)
    other = lax.ppermute(mine, "col", swap)

    quarter = tall((window // 4, cols_here), BF16)
    left, *sent = call(
        functools.partial(first_kernel, rows), (tall((window, rows_here), BF16), quarter, quarter), work
    )(in_specs=[SMEM, VMEM, VMEM, VMEM])(where, mine, other, sparse)
    last, kept = call(second_kernel, (quarter, tall(quarter.shape, F32)), work)(in_specs=[SMEM, VMEM, VMEM])(
        where, left, sparse
    )
    got = [
        lax.ppermute(part, BOTH, pairs([(z, step) for z in range(rows)]))
        for part, step in zip((*sent, last), STEPS)
    ]
    ready = call(functools.partial(order_kernel, groups), quarter, 10**6)(in_specs=[SMEM] + [VMEM] * 4)(
        where, kept, *got
    )
    parts = lax.all_to_all(ready.reshape(groups, piece, cols_here), "row", 0, 0, axis_index_groups=strided, tiled=True)
    result = parts.astype(F32).sum(0)
    result = result * mask(cols_here // BS, row * piece // BS, col * (cols_here // BS))
    return result.astype(BF16)


def solution(mesh):
    rows, cols = mesh.shape["row"], mesh.shape["col"]
    return jax.shard_map(
        functools.partial(body, rows, cols),
        mesh=mesh,
        in_specs=(P("row", "col"), P("row", "col"), P()),
        out_specs=P("row", "col"),
        check_vma=False,
    )
```

```python
import functools

import jax
import jax.numpy as jnp
from jax import lax
from jax.experimental import pallas as pl
from jax.experimental.pallas import tpu as pltpu
from jax.sharding import PartitionSpec as P

BS = 128
BF16 = jnp.bfloat16
F32 = jnp.float32
VMEM = pl.BlockSpec(memory_space=pltpu.VMEM)
SMEM = pl.BlockSpec(memory_space=pltpu.SMEM)
BOTH = ("row", "col")
STEPS = (2, 1, -1, 0)


def call(kernel, outs, cost):
    return functools.partial(
        pl.pallas_call,
        kernel,
        out_shape=outs,
        out_specs=jax.tree.map(lambda _: VMEM, outs),
        compiler_params=pltpu.CompilerParams(vmem_limit_bytes=24 * 2**20),
        cost_estimate=pl.CostEstimate(flops=cost, bytes_accessed=4 * 2**20, transcendentals=0),
    )


def panel_kernel(where_ref, occ_ref, window_ref, mine_ref, sent_ref):
    core = where_ref[1] % 2
    blocks = mine_ref.shape[0] // BS

    @pl.when(where_ref[0] != 0)
    def _():
        mine_ref[...] = jnp.zeros_like(mine_ref)
        sent_ref[...] = jnp.zeros_like(sent_ref)

    @pl.when(where_ref[0] == 0)
    def _():
        for half, out_ref in ((core, mine_ref), (1 - core, sent_ref)):
            for i in range(blocks):
                down = half * blocks + i
                rows = pl.ds(pl.multiple_of(down * BS, BS), BS)
                for j in range(occ_ref.shape[1]):
                    across = pl.ds(j * BS, BS)
                    kept = window_ref[rows, across] * occ_ref[down, j].astype(F32).astype(BF16)
                    out_ref[pl.ds(i * BS, BS), across] = kept


def mask_kernel(occ_ref, density_ref, sparse_ref):
    for i in range(occ_ref.shape[0]):
        for j in range(occ_ref.shape[1]):
            spot = (pl.ds(i * BS, BS), pl.ds(j * BS, BS))
            sparse_ref[spot] = density_ref[spot] * occ_ref[i, j].astype(F32).astype(BF16)


def square_part(left_ref, sparse_ref, n):
    return lax.dot_general(
        left_ref[...], sparse_ref[n, :], (((1,), (1,)), ((), ())), preferred_element_type=F32
    )


def tiles(size):
    tile = min(256, size)
    return [pl.ds(n, tile) for n in range(0, size, tile)]


def own_kernel(left_ref, sparse_ref, total_ref):
    for n in tiles(sparse_ref.shape[0]):
        total_ref[:, n] = square_part(left_ref, sparse_ref, n)


def both_kernel(left_ref, sparse_ref, total_ref, out_ref):
    for n in tiles(sparse_ref.shape[0]):
        out_ref[:, n] = (total_ref[:, n] + square_part(left_ref, sparse_ref, n)).astype(BF16)


def cube_part(where_ref, left_ref, sparse_ref, first, *out_refs):
    three = jnp.where(where_ref[0] == where_ref[1], 3.0, 0.0).astype(F32)
    size = out_refs[0].shape[0]
    rows = pl.ds(first, len(out_refs) * size)
    for n in tiles(out_refs[0].shape[1]):
        product = jnp.dot(left_ref[rows, :], sparse_ref[:, n], preferred_element_type=F32)
        total = three * left_ref[rows, n].astype(F32) - 2.0 * product
        for i, out_ref in enumerate(out_refs):
            out_ref[:, n] = total[i * size : (i + 1) * size].astype(out_ref.dtype)


def first_kernel(rows, where_ref, mine_ref, other_ref, sparse_ref, left_ref, *sent_refs):
    row, core = where_ref[0], where_ref[1] % 2
    sign = 1 - 2 * core
    piece = left_ref.shape[0] // rows
    half = rows // 2
    order = [(t + rows) % rows for start in STEPS for t in range(start, start + rows, 4)]
    for place, t in enumerate(order):
        target = (row + sign * t + rows) % rows
        source = pl.ds(pl.multiple_of((target % half) * piece, piece), piece)
        spot = pl.ds(place * piece, piece)
        left_ref[spot, :] = jnp.where(target // half == core, mine_ref[source, :], other_ref[source, :])
    cube_part(where_ref, left_ref, sparse_ref, 0, *sent_refs)


def second_kernel(where_ref, left_ref, sparse_ref, kept_ref):
    cube_part(where_ref, left_ref, sparse_ref, left_ref.shape[0] - kept_ref.shape[0], kept_ref)


def spread(member, groups):
    return (member + (1 - member % 2) * (groups // 2)) % groups if groups % 4 == 0 else member


def order_kernel(groups, where_ref, kept_ref, *refs):
    *got_refs, out_ref = refs
    row, col = where_ref[0], where_ref[1]
    sign = 1 - 2 * (col % 2)
    piece = out_ref.shape[0] // groups
    for u in range(groups):
        place = spread((row // 4 + sign * u + groups) % groups, groups)
        source = pl.ds(u * piece, piece)
        total = kept_ref[source, :]
        for got_ref in got_refs:
            total += got_ref[source, :].astype(F32)
        out_ref[pl.ds(pl.multiple_of(place * piece, piece), piece), :] = total.astype(BF16)


def body(rows, cols, density, occupancy, product_keep):
    rows_here, cols_here = density.shape
    window = product_keep.shape[0] * BS
    row, col = lax.axis_index("row"), lax.axis_index("col")
    where = jnp.stack([row, col]).astype(jnp.int32)
    half = window // 2
    piece = window // rows
    chips = cols // 2
    tall = jax.ShapeDtypeStruct
    work = window * rows_here * cols_here

    def pairs(moves, way=1):
        return [
            (z * sign % rows * cols + c, (z + step) * sign % rows * cols + c)
            for z, step in moves
            for c in range(cols)
            for sign in [way * (1 - 2 * (c % 2))]
        ]

    same_core = [[2 * i + k for i in range(chips)] for k in range(2)]
    groups = rows // 4
    members = sorted(range(groups), key=lambda i: spread(i, groups))
    strided = [[4 * i + o for i in members] for o in range(4)]

    def mask(across, down_first, across_first):
        kept = lax.dynamic_slice(product_keep, (down_first, across_first), (1, across))
        return jnp.repeat(kept, BS, axis=1).astype(F32)

    swap = [(c, c ^ 1) for c in range(cols)]
    mine, sent = call(
        panel_kernel,
        [tall((half, cols_here), BF16)] * 2,
        10**6,
    )(in_specs=[SMEM, SMEM, VMEM])(where, occupancy, density[:window])
    halves = [mine, lax.ppermute(sent, BOTH, swap)]
    sparse = call(mask_kernel, tall(density.shape, BF16), 10**6)(in_specs=[SMEM, VMEM])(occupancy, density)
    sibling = lax.ppermute(sparse, "col", swap)
    far = rows // 4
    have, gap, stages = [-far, 0, far, 2 * far], far, []
    while gap > 2:
        gap //= 4
        stages.append([(z, gap) for z in have])
        stages.append([(z, -gap) for z in have] + [(z + gap, gap) for z in have])
        have = [z + step * gap for z in have for step in (-1, 0, 1, 2)]
    stages.append([(z, 1) for z in have])
    spread_out = []
    for h, way in zip(halves, (1, -1)):
        near = h + lax.ppermute(h, BOTH, pairs([(0, far)], way))
        back = lax.ppermute(h, BOTH, pairs([(0, -far)], way))
        spread_out.append(near + back + lax.ppermute(near, BOTH, pairs([(far, far)], way)))
    halves = spread_out
    for moves in stages:
        halves = [h + lax.ppermute(h, BOTH, pairs(moves, way)) for h, way in zip(halves, (1, -1))]

    total = call(own_kernel, tall((half, rows_here), F32), work)(in_specs=[VMEM] * 2)(halves[0], sparse)
    kept = call(both_kernel, tall((half, rows_here), BF16), work)(in_specs=[VMEM] * 3)(halves[1], sibling, total)
    parts = lax.all_to_all(kept.reshape(chips, piece, rows_here), "col", 0, 0, axis_index_groups=same_core, tiled=True)
    first = (col % 2) * half + (col // 2) * piece
    square = parts.astype(F32).sum(0) * mask(rows_here // BS, first // BS, row * (rows_here // BS))
    square = jnp.broadcast_to(square.astype(BF16), (chips, piece, rows_here))
    mine = lax.all_to_all(square, "col", 0, 0, axis_index_groups=same_core, tiled=True).reshape(half, rows_here)
    other = lax.ppermute(mine, "col", swap)

    quarter = tall((window // 4, cols_here), BF16)
    left, *sent = call(
        functools.partial(first_kernel, rows), (tall((window, rows_here), BF16), *[quarter] * 3), work
    )(in_specs=[SMEM, VMEM, VMEM, VMEM])(where, mine, other, sparse)
    kept = call(second_kernel, tall(quarter.shape, F32), work)(in_specs=[SMEM, VMEM, VMEM])(where, left, sparse)
    got = [
        lax.ppermute(part, BOTH, pairs([(z, step) for z in range(rows)]))
        for part, step in zip(sent, STEPS)
    ]
    ready = call(functools.partial(order_kernel, groups), quarter, 10**6)(in_specs=[SMEM] + [VMEM] * 4)(
        where, kept, *got
    )
    parts = lax.all_to_all(ready.reshape(groups, piece, cols_here), "row", 0, 0, axis_index_groups=strided, tiled=True)
    result = parts.astype(F32).sum(0)
    result = result * mask(cols_here // BS, row * piece // BS, col * (cols_here // BS))
    return result.astype(BF16)


def solution(mesh):
    rows, cols = mesh.shape["row"], mesh.shape["col"]
    return jax.shard_map(
        functools.partial(body, rows, cols),
        mesh=mesh,
        in_specs=(P("row", "col"), P("row", "col"), P()),
        out_specs=P("row", "col"),
        check_vma=False,
    )
```
